32 devices in a mesh: dp: 8 (over z, y), tensor: 4 (over x, core).
Axes of the slice: x: 2, y: 2, z: 4, core: 2. Of those that a mesh axis runs over, the one named last changes fastest.
Arguments:
- tokens: bfloat16 [1024, 3072], P('dp', 'tensor'), may hold values from -6 to 6
- grad_out: bfloat16 [1024, 3072], P('dp', 'tensor'), may hold values from -6 to 6
- expert_ids: int32 [1024, 2], P('dp'), may hold values from 0 to 7, as said below
- gate_probs: float32 [1024, 2], P('dp'), may hold values from 0.2 to 1
- w_gate: bfloat16 [8, 3072, 8192], P('dp', None, 'tensor'), may hold values from -0.109375 to 0.109375
- w_up: bfloat16 [8, 3072, 8192], P('dp', None, 'tensor'), may hold values from -0.109375 to 0.109375
- w_down: bfloat16 [8, 8192, 3072], P('dp', 'tensor'), may hold values from -0.0625 to 0.0625
Outputs:
- input_grad: bfloat16 [1024, 3072], P('dp', 'tensor')
- grad_gate: bfloat16 [8, 3072, 8192], P('dp', None, 'tensor')
- grad_up: bfloat16 [8, 3072, 8192], P('dp', None, 'tensor')
- grad_down: bfloat16 [8, 8192, 3072], P('dp', 'tensor')
The draws below stay inside these ranges and needn't reach their ends.
Inputs may be any that keep to these rules, and one draw needn't show every extreme that they name: `expert_ids`: A token's two experts differ. Among the 128 tokens of one index of dp (aligned blocks of rows), no expert is named more than 33 times, and one expert, the same in every block, is named exactly 33 times in each block.
All inputs are finite; a program needn't handle non-finite values.
Results may differ from the reference program's by a relative error of at most 0.015.
Values may be sent and summed in bfloat16 or wider, within the bound.
No kernel may reach another device: no remote copies, remote signals or barrier semaphores. Data moves between devices by JAX's collectives and lax.ppermute only.
A program may use at most 192 MiB of HBM per device.

```python
import jax
import jax.numpy as jnp
from jax import lax

D = 3072
FF = 8192
EXPERTS = 8
TOP = 2
TOK_DEV = 128
CAP = 33
TOKENS = 1024
SLICES = 1
FF_DEV = 2048
N_DP = 8
N_TENSOR = 4


def route_block(key, hot_expert):
    key_perm, key_jitter, key_order, key_swap = jax.random.split(key, 4)
    others = jax.random.permutation(key_perm, EXPERTS - 1).astype(jnp.int32)
    others = jnp.where(others >= hot_expert, others + 1, others)
    spare_slots = 2 * TOK_DEV - CAP
    base_count = spare_slots // (EXPERTS - 1)
    extra_count = spare_slots % (EXPERTS - 1)
    jitter = CAP - base_count - 1
    halves = (EXPERTS - 1) // 2
    shifts = jax.random.randint(key_jitter, (halves,), 0, jitter + 1).astype(jnp.int32)
    changes = jnp.concatenate([shifts, -shifts, jnp.zeros((EXPERTS - 1 - 2 * halves,), jnp.int32)])
    counts = base_count + (jnp.arange(EXPERTS - 1) < extra_count).astype(jnp.int32) + changes
    sizes_all = jnp.concatenate([jnp.full((1,), CAP, jnp.int32), counts.astype(jnp.int32)])
    group_order = jnp.concatenate([jnp.reshape(hot_expert, (1,)), others])
    bounds = jnp.cumsum(sizes_all)
    places = jnp.arange(2 * TOK_DEV, dtype=jnp.int32)
    group_index = jnp.sum((places[:, None] >= bounds[None, :]).astype(jnp.int32), axis=1)
    chosen = group_order[group_index]
    first_pick = chosen[:TOK_DEV]
    second_pick = chosen[TOK_DEV:]
    swap_flags = jax.random.randint(key_swap, (TOK_DEV,), 0, 2)
    pairing = jnp.where(swap_flags[:, None] == 1, jnp.stack([second_pick, first_pick], axis=1), jnp.stack([first_pick, second_pick], axis=1))
    token_order = jax.random.permutation(key_order, TOK_DEV)
    return pairing[token_order]


def draw_expert_ids(key, part):
    key_hot, key_blocks = jax.random.split(jax.random.fold_in(key, 17), 2)
    hot_expert = jax.random.randint(key_hot, (), 0, EXPERTS).astype(jnp.int32)
    block_keys = jax.random.split(key_blocks, TOKENS // TOK_DEV)
    blocks = jax.vmap(route_block, in_axes=(0, None))(block_keys, hot_expert)
    return blocks.reshape(TOKENS, TOP).astype(jnp.int32)


def steps_of(stream_key, dims, shards, low, top_value):
    loudness = 1.0
    for dim, shards_of in shards:
        steps = jax.random.uniform(jax.random.fold_in(jax.random.fold_in(stream_key, 6), dim), (shards_of,), jnp.float32, low / len(shards), top_value / len(shards))
        loudness = loudness * jnp.repeat(jnp.exp(steps), dims[dim] // shards_of).reshape((-1,) + (1,) * (len(dims) - 1 - dim))
    return loudness


def normal_values(stream_key, shape, width, reach, cuts=(), kind=jnp.bfloat16):
    factor_of = steps_of(stream_key, shape, cuts, -0.22, 0.18) if cuts else 1.0
    array = jax.random.normal(stream_key, shape, jnp.float32) * width * factor_of
    return jnp.minimum(jnp.maximum(array, -reach), reach).astype(kind)


def setup_inputs(seed: int = 0) -> dict:
    arg_keys = jax.random.split(jax.random.key(seed), 8)
    return {
        "tokens": normal_values(arg_keys[0], (TOKENS, D), 1.0, 6.0, ((0, 8), (1, 4))),
        "grad_out": normal_values(arg_keys[1], (TOKENS, D), 1.0, 6.0, ((0, 8), (1, 4))),
        "expert_ids": draw_expert_ids(jax.random.fold_in(arg_keys[7], 71), 0),
        "gate_probs": jnp.clip(0.2 + 0.8 * jax.random.uniform(arg_keys[3], (TOKENS, TOP), jnp.float32) ** steps_of(arg_keys[3], (TOKENS, TOP), ((0, 8),), -0.2, 0.2), 0.2, 1.0),
        "w_gate": normal_values(arg_keys[4], (EXPERTS * SLICES, D, FF // SLICES), D ** -0.5, 0.109375, ((0, 8), (2, 4))),
        "w_up": normal_values(arg_keys[5], (EXPERTS * SLICES, D, FF // SLICES), D ** -0.5, 0.109375, ((0, 8), (2, 4))),
        "w_down": normal_values(arg_keys[6], (EXPERTS * SLICES, FF // SLICES, D), FF ** -0.5, 0.0625, ((0, 8), (1, 4))),
    }


def block_sum(gate_grad, up_grad, gate_full, up_full):
    def add_block(block, running):
        start = block * FF_DEV
        gate_piece = lax.dynamic_slice_in_dim(gate_grad, start, FF_DEV, 1)
        up_piece = lax.dynamic_slice_in_dim(up_grad, start, FF_DEV, 1)
        gate_rows = lax.dynamic_slice_in_dim(gate_full, start, FF_DEV, 1)
        up_rows = lax.dynamic_slice_in_dim(up_full, start, FF_DEV, 1)
        part = jnp.dot(gate_piece, gate_rows.T, preferred_element_type=jnp.float32)
        part = part + jnp.dot(up_piece, up_rows.T, preferred_element_type=jnp.float32)
        rounded = lax.optimization_barrier(part.astype(jnp.bfloat16))
        return running + rounded.astype(jnp.float32)

    start_value = jnp.zeros((gate_grad.shape[0], D), jnp.float32)
    return lax.fori_loop(0, SLICES * N_TENSOR, add_block, start_value)


def reference(tokens, grad_out, expert_ids, gate_probs, w_gate, w_up, w_down):
    pair_count = TOKENS * TOP
    flat_ids = expert_ids.reshape(-1).astype(jnp.int32)
    experts_row = jnp.arange(EXPERTS, dtype=jnp.int32)
    onehot = (flat_ids[:, None] == experts_row[None, :]).astype(jnp.int32)
    rank_index = jnp.sum((jnp.cumsum(onehot, axis=0) - onehot) * onehot, axis=1).astype(jnp.int32)
    rows_most = N_DP * CAP
    lookup = jnp.full((EXPERTS, rows_most), pair_count, jnp.int32)
    lookup = lookup.at[flat_ids, rank_index].set(jnp.arange(pair_count, dtype=jnp.int32))
    token_rows = jnp.concatenate([tokens, jnp.zeros((1, D), jnp.bfloat16)], axis=0)
    scaled = (gate_probs[:, :, None] * grad_out[:, None, :].astype(jnp.float32)).astype(jnp.bfloat16)
    scaled = jnp.concatenate([scaled.reshape(pair_count, D), jnp.zeros((1, D), jnp.bfloat16)], axis=0)
    input_total = jnp.zeros((TOKENS + 1, D), jnp.float32)
    gate_list = []
    up_list = []
    down_list = []
    for expert in range(EXPERTS):
        chosen = lookup[expert]
        token_index = jnp.where(chosen < pair_count, chosen // TOP, TOKENS).astype(jnp.int32)
        expert_rows = token_rows[token_index]
        expert_grads = scaled[chosen]
        first_row = expert * SLICES
        gate_full = jnp.transpose(w_gate[first_row:first_row + SLICES], (1, 0, 2)).reshape(D, FF)
        up_full = jnp.transpose(w_up[first_row:first_row + SLICES], (1, 0, 2)).reshape(D, FF)
        down_full = w_down[first_row:first_row + SLICES].reshape(FF, D)
        gate_value = jnp.dot(expert_rows, gate_full, preferred_element_type=jnp.float32)
        up_value = jnp.dot(expert_rows, up_full, preferred_element_type=jnp.float32)
        sigmoid_value = jax.nn.sigmoid(gate_value)
        silu_value = gate_value * sigmoid_value
        hidden = (silu_value * up_value).astype(jnp.bfloat16)
        hidden_grad = jnp.dot(expert_grads, down_full.T, preferred_element_type=jnp.float32)
        gate_grad = (hidden_grad * up_value * sigmoid_value * (1.0 + gate_value * (1.0 - sigmoid_value))).astype(jnp.bfloat16)
        up_grad = (hidden_grad * silu_value).astype(jnp.bfloat16)
        row_grads = block_sum(gate_grad, up_grad, gate_full, up_full)
        input_total = input_total.at[token_index].add(row_grads)
        gate_total = jnp.dot(expert_rows.T, gate_grad, preferred_element_type=jnp.float32)
        up_total = jnp.dot(expert_rows.T, up_grad, preferred_element_type=jnp.float32)
        down_total = jnp.dot(hidden.T, expert_grads, preferred_element_type=jnp.float32)
        gate_list.append(jnp.transpose(gate_total.reshape(D, SLICES, FF // SLICES), (1, 0, 2)).astype(jnp.bfloat16))
        up_list.append(jnp.transpose(up_total.reshape(D, SLICES, FF // SLICES), (1, 0, 2)).astype(jnp.bfloat16))
        down_list.append(down_total.reshape(SLICES, FF // SLICES, D).astype(jnp.bfloat16))
    input_grad = input_total[:TOKENS].astype(jnp.bfloat16)
    grad_gate = jnp.concatenate(gate_list, axis=0)
    grad_up = jnp.concatenate(up_list, axis=0)
    grad_down = jnp.concatenate(down_list, axis=0)
    return (input_grad, grad_gate, grad_up, grad_down)
```

```python
import functools

import jax
import jax.numpy as jnp
from jax import lax
from jax.experimental import pallas as pl
from jax.experimental.pallas import tpu as pltpu
from jax.sharding import PartitionSpec as P

EXPERTS = 8
TOP = 2
CAP = 33
MAIN = 32
LANES = 128
BF16 = jnp.bfloat16
F32 = jnp.float32
MIB = 1 << 20


def dot(left, right, left_dim, right_dim):
    return lax.dot_general(
        left, right, (((left_dim,), (right_dim,)), ((), ())), preferred_element_type=F32
    )


def message_rows(width):
    blocks = width // LANES
    return blocks * MAIN + -(-blocks // 8) * 8


def lanes(start):
    return pl.ds(pl.multiple_of(start, LANES), LANES)


def select_rows(ids):
    count = ids.shape[1]
    expert = lax.broadcasted_iota(jnp.int32, (EXPERTS, count), 0)
    hit = ids[0:1] == expert
    for choice in range(1, TOP):
        hit = hit | (ids[choice : choice + 1] == expert)
    earlier = lax.broadcasted_iota(jnp.int32, (count, count), 0) < lax.broadcasted_iota(
        jnp.int32, (count, count), 1
    )
    rank = dot(hit.astype(F32).astype(BF16), earlier.astype(F32).astype(BF16), 1, 0)
    rank = jnp.where(hit, rank, -1.0)
    place = lax.broadcasted_iota(jnp.int32, (MAIN, count), 0).astype(F32)
    rows = [(rank[e : e + 1] == place).astype(F32) for e in range(EXPERTS)]
    rows.append((rank == float(MAIN)).astype(F32))
    return jnp.concatenate(rows, axis=0)


def row_weights(ids, probs, picks):
    count = ids.shape[1]
    expert = lax.broadcasted_iota(jnp.int32, (EXPERTS, count), 0)
    weight = jnp.zeros((EXPERTS, count), F32)
    for choice in range(TOP):
        weight = weight + jnp.where(
            ids[choice : choice + 1] == expert, probs[choice : choice + 1], 0.0
        )
    spread = [jnp.broadcast_to(weight[e : e + 1], (MAIN, count)) for e in range(EXPERTS)]
    spread = jnp.concatenate(spread + [weight], axis=0)
    return jnp.sum(spread * picks, axis=1, keepdims=True)


def pack(out_ref, rows):
    count, width = out_ref.shape[0], rows.shape[1]
    blocks = width // LANES
    left = out_ref.shape[1] - blocks * MAIN
    for i in range(count):
        for c in range(blocks):
            piece = rows[i * MAIN : (i + 1) * MAIN, c * LANES : (c + 1) * LANES]
            out_ref[i, c * MAIN : (c + 1) * MAIN, :] = piece.astype(BF16)
        last = rows[count * MAIN + i : count * MAIN + i + 1]
        lines = [last[:, c * LANES : (c + 1) * LANES] for c in range(blocks)]
        lines.append(jnp.zeros((left - blocks, LANES), F32))
        out_ref[i, blocks * MAIN :, :] = jnp.concatenate(lines, axis=0).astype(BF16)


def unpack(out_ref, message_ref, width, start):
    count = message_ref.shape[0]
    blocks = width // LANES
    last = [message_ref[i, blocks * MAIN :, :].astype(F32) for i in range(count)]
    for c in range(blocks):
        place = lanes(start + c * LANES)
        for i in range(count):
            out_ref[i * MAIN : (i + 1) * MAIN, place] = message_ref[i, c * MAIN : (c + 1) * MAIN, :]
        lines = jnp.concatenate([piece[c : c + 1] for piece in last], axis=0)
        out_ref[count * MAIN :, place] = lines.astype(BF16)


def vmem_spec():
    return pl.BlockSpec(memory_space=pltpu.VMEM)


def smem_spec():
    return pl.BlockSpec(memory_space=pltpu.SMEM)


def params(mib):
    return pltpu.CompilerParams(vmem_limit_bytes=mib * MIB)


def cost(flops, nbytes):
    return pl.CostEstimate(flops=int(flops), bytes_accessed=int(nbytes), transcendentals=0)


def whole(shape):
    return pl.BlockSpec(shape, lambda i: (0,) * len(shape), pipeline_mode=pl.Buffered(1))


def in_hbm(array):
    return pltpu.with_memory_space_constraint(array, pltpu.HBM)


def pack_messages(ids, probs, tokens, grads):
    def body(ids_ref, probs_ref, tokens_ref, grads_ref, token_out, grad_out):
        ids_in = ids_ref[...]
        picks = select_rows(ids_in)
        scale = row_weights(ids_in, probs_ref[...], picks)
        picks = picks.astype(BF16)
        pack(token_out, dot(picks, tokens_ref[...], 1, 0))
        pack(grad_out, dot(picks, grads_ref[...], 1, 0) * scale)

    shape = (EXPERTS, message_rows(grads.shape[1]), LANES)
    arrays = (ids, probs, tokens, grads)
    return pl.pallas_call(
        body,
        grid=(1,),
        in_specs=[whole(array.shape) for array in arrays],
        out_specs=[whole(shape)] * 2,
        out_shape=[jax.ShapeDtypeStruct(shape, BF16)] * 2,
        compiler_params=params(8),
        name="pack_messages",
    )(*[in_hbm(array) for array in arrays])


def combine(ids, messages, slices, width):
    count = ids.shape[1]

    def body(ids_ref, message_ref, out_ref, rows_ref):
        picks = select_rows(ids_ref[...]).astype(BF16)
        total = jnp.zeros((count, width), F32)
        for s in range(slices):
            unpack(rows_ref, message_ref.at[s], width, 0)
            total = total + dot(picks, rows_ref[...], 0, 0)
        out_ref[...] = total.astype(BF16)

    return pl.pallas_call(
        body,
        in_specs=[vmem_spec()] * 2,
        out_specs=vmem_spec(),
        out_shape=jax.ShapeDtypeStruct((count, width), BF16),
        scratch_shapes=[pltpu.VMEM((EXPERTS * CAP, width), BF16)],
        compiler_params=params(16),
        name="combine",
    )(ids, messages)


IN_FLIGHT = 13 * MIB


class Stream:
    def __init__(self, *groups):
        self.copies, self.blocks, self.sizes, self.before = [], [], [], []
        for sources, held, sems in groups:
            slots, first = held.shape[0], len(self.copies)
            for i, source in enumerate(sources):
                slot = i % slots
                self.copies.append(pltpu.make_async_copy(source, held.at[slot], sems.at[slot]))
                self.blocks.append(held.at[slot])
                self.sizes.append(2 * held.shape[1] * held.shape[2])
                self.before.append(first + i - slots if i >= slots else -1)
        self.started = self.arrived = self.used = 0
        self.start()

    def start(self):
        while self.started < len(self.copies):
            flying = sum(self.sizes[self.arrived : self.started + 1])
            if self.before[self.started] >= self.used or flying > IN_FLIGHT:
                break
            self.copies[self.started].start()
            self.started += 1

    def next(self, count):
        self.used = self.arrived
        self.start()
        first = self.arrived
        for i in range(first, first + count):
            if i >= self.started:
                self.copies[i].start()
                self.started += 1
            self.copies[i].wait()
        self.arrived += count
        self.start()
        return self.blocks[first : first + count]


def buffers(slots, *block):
    return [pltpu.VMEM((slots, *block), BF16), pltpu.SemaphoreType.DMA((slots,))]


def feature_block(ref, index, k, width, cols):
    start = pl.multiple_of((index ^ k) * width, LANES)
    return ref.at[0, pl.ds(start, width), cols]


def feature_cols(ref, index, k, width, rows):
    start = pl.multiple_of((index ^ k) * width, LANES)
    return ref.at[0, rows, pl.ds(start, width)]


def chunk_of(total):
    return min(512, total)


def chunks(total):
    step = chunk_of(total)
    return [pl.ds(j, step) for j in range(0, total, step)]


def any_specs(count):
    return [pl.BlockSpec(memory_space=pl.ANY)] * count


def gate_up_first(index, parts, w_gate, w_up, rows, width):
    hidden_units = w_gate.shape[2]
    n = len(parts)

    def body(index_ref, *refs):
        part_refs = refs[:n]
        w_gate_ref, w_up_ref, gate_ref, up_ref, x_ref, held_ref, sems = refs[n:]
        at = index_ref[0]
        sources = [
            feature_block(ref, at, k, width, cols)
            for cols in chunks(hidden_units)
            for ref in (w_gate_ref, w_up_ref)
            for k in range(n)
        ]
        stream = Stream((sources, held_ref, sems))
        for k in range(n):
            unpack(x_ref, part_refs[k], width, k * width)
        for cols in chunks(hidden_units):
            blocks = stream.next(2 * n)
            for i, out_ref in enumerate((gate_ref, up_ref)):
                value = None
                for k in range(n):
                    more = dot(x_ref[:, k * width : (k + 1) * width], blocks[i * n + k][...], 1, 0)
                    value = more if value is None else value + more
                out_ref[:, cols] = value

    wide = jax.ShapeDtypeStruct((rows, hidden_units), F32)
    return pl.pallas_call(
        body,
        grid=(1,),
        in_specs=[smem_spec()] + [whole(part.shape) for part in parts] + any_specs(2),
        out_specs=[vmem_spec()] * 2,
        out_shape=[wide, wide],
        scratch_shapes=[
            pltpu.VMEM((rows, n * width), BF16),
            *buffers(6 * n, width, chunk_of(hidden_units)),
        ],
        compiler_params=params(20),
        cost_estimate=cost(
            4 * n * rows * width * hidden_units, 4 * n * width * hidden_units
        ),
        name="gate_up_first",
    )(index, *parts, in_hbm(w_gate), in_hbm(w_up))


def hidden_state(index, parts, gate_up, w_gate, w_up, rows, width):
    hidden_units = w_gate.shape[2]
    n = len(parts)
    early = 2
    late = n - early

    def body(index_ref, *refs):
        part_refs = refs[:n]
        gate_in, up_in, w_gate_ref, w_up_ref, x_out, hidden_out = refs[n : n + 6]
        slope_ref, silu_ref, x_ref, hidden_ref, held_ref, sems, out_sems = refs[n + 6 :]
        at = index_ref[0]
        sources = [
            feature_block(ref, at, k, width, cols)
            for cols in chunks(hidden_units)
            for ref in (w_gate_ref, w_up_ref)
            for k in range(early, n)
        ]
        stream = Stream((sources, held_ref, sems))
        for k in range(n):
            unpack(x_ref, part_refs[k], width, (at ^ k) * width)
        x_copy = pltpu.make_async_copy(x_ref, x_out, out_sems.at[0])
        x_copy.start()
        for cols in chunks(hidden_units):
            values = []
            blocks = stream.next(2 * late)
            for i, before in enumerate((gate_in, up_in)):
                value = before[:, cols]
                for k in range(early, n):
                    place = pl.ds(pl.multiple_of((at ^ k) * width, LANES), width)
                    block = blocks[i * late + k - early]
                    value = value + dot(x_ref[:, place], block[...], 1, 0)
                values.append(value)
            gate, up = values
            sig = jax.nn.sigmoid(gate)
            silu = gate * sig
            hidden_ref[:, cols] = (silu * up).astype(BF16)
            slope_ref[:, cols] = (up * sig * (1.0 + gate * (1.0 - sig))).astype(BF16)
            silu_ref[:, cols] = silu.astype(BF16)
        hidden_copy = pltpu.make_async_copy(hidden_ref, hidden_out, out_sems.at[1])
        hidden_copy.start()
        x_copy.wait()
        hidden_copy.wait()

    wide = (rows, hidden_units)
    return pl.pallas_call(
        body,
        grid=(1,),
        in_specs=[smem_spec()]
        + [whole(part.shape) for part in parts]
        + [vmem_spec()] * 2
        + any_specs(2),
        out_specs=any_specs(2) + [vmem_spec()] * 2,
        out_shape=[
            pltpu.HBM((rows, n * width), BF16),
            pltpu.HBM(wide, BF16),
            jax.ShapeDtypeStruct(wide, BF16),
            jax.ShapeDtypeStruct(wide, BF16),
        ],
        scratch_shapes=[
            pltpu.VMEM((rows, n * width), BF16),
            pltpu.VMEM(wide, BF16),
            *buffers(6 * late, width, chunk_of(hidden_units)),
            pltpu.SemaphoreType.DMA((2,)),
        ],
        compiler_params=params(24),
        cost_estimate=cost(
            4 * late * rows * width * hidden_units, 4 * late * width * hidden_units
        ),
        name="hidden_state",
    )(index, *parts, *gate_up, in_hbm(w_gate), in_hbm(w_up))


def early_grads(index, parts, w_down, early, after, rows, width):
    hidden_units = w_down.shape[1]
    n = len(parts)
    late = w_down.shape[2] // width - early

    def body(index_ref, *refs):
        part_refs = refs[:n]
        w_down_ref, _, grad_ref, late_ref, y_ref, held_ref, sems, late_sems = refs[n:]
        at = index_ref[0]
        stream = Stream(
            (
                [
                    feature_cols(w_down_ref, at, k, width, cols)
                    for cols in chunks(hidden_units)
                    for k in range(early)
                ],
                held_ref,
                sems,
            )
        )
        copies = [
            pltpu.make_async_copy(
                feature_cols(w_down_ref, at, early + k, width, slice(None)),
                late_ref.at[k],
                late_sems.at[k],
            )
            for k in range(late)
        ]
        for k in range(n):
            unpack(y_ref, part_refs[k], width, k * width)
        for i, cols in enumerate(chunks(hidden_units)):
            blocks = stream.next(early)
            if i == 0:
                for copy in copies:
                    copy.start()
            value = None
            for k in range(early):
                more = dot(y_ref[:, k * width : (k + 1) * width], blocks[k][...], 1, 1)
                value = more if value is None else value + more
            grad_ref[:, cols] = value
        for copy in copies:
            copy.wait()

    return pl.pallas_call(
        body,
        grid=(1,),
        in_specs=[smem_spec()] + [whole(part.shape) for part in parts] + any_specs(2),
        out_specs=[vmem_spec()] * 2,
        out_shape=[
            jax.ShapeDtypeStruct((rows, hidden_units), F32),
            pltpu.VMEM((late, hidden_units, width), BF16),
        ],
        scratch_shapes=[
            pltpu.VMEM((rows, early * width), BF16),
            *buffers(4 * early, chunk_of(hidden_units), width),
            pltpu.SemaphoreType.DMA((late,)),
        ],
        compiler_params=params(16),
        cost_estimate=cost(
            2 * early * rows * width * hidden_units, 4 * early * width * hidden_units
        ),
        name="early_grads",
    )(index, *parts, in_hbm(w_down), after)


def input_parts(index, grads, early, grad_early, w_late, slope, silu, w_gate, w_up, rows, width):
    hidden_units = w_gate.shape[2]
    n = len(grads)
    count, lines = grads[0].shape[:2]
    order = list(range(n - 1, 0, -2)) + list(range(n - 2, -1, -2))
    step = 256 if width % 256 == 0 else LANES

    def body(index_ref, *refs):
        part_refs = refs[:n]
        grad_in, late_ref, slope_ref, silu_ref, w_gate_ref, w_up_ref = refs[n : n + 6]
        y_out, gate_ref, up_ref, odd_ref, even_ref = refs[n + 6 : n + 11]
        y_ref, rows_ref, held_ref, sems, out_sem = refs[n + 11 :]
        at = index_ref[0]
        sources = [
            feature_block(ref, at, k, width, slice(None))
            for k in order
            for ref in (w_gate_ref, w_up_ref)
        ]
        stream = Stream((sources, held_ref, sems))
        for k in range(n):
            unpack(y_ref, part_refs[k], width, (at ^ k) * width)
        y_copy = pltpu.make_async_copy(y_ref, y_out, out_sem)
        y_copy.start()
        for cols in chunks(hidden_units):
            grad = grad_in[:, cols]
            for k in range(early, n):
                place = pl.ds(pl.multiple_of((at ^ k) * width, LANES), width)
                grad = grad + dot(y_ref[:, place], late_ref[k - early, cols, :], 1, 1)
            gate_ref[:, cols] = (grad * slope_ref[:, cols].astype(F32)).astype(BF16)
            up_ref[:, cols] = (grad * silu_ref[:, cols].astype(F32)).astype(BF16)
        for i in range(n):
            gate_block, up_block = stream.next(2)
            for j in range(0, width, step):
                value = dot(gate_ref[...], gate_block[j : j + step, :], 1, 1)
                value = value + dot(up_ref[...], up_block[j : j + step, :], 1, 1)
                rows_ref[:, j : j + step] = value
            out_ref = odd_ref if i < n // 2 else even_ref
            pack(out_ref.at[i % (n // 2)], rows_ref[...])
        y_copy.wait()

    wide = jax.ShapeDtypeStruct((rows, hidden_units), BF16)
    messages = jax.ShapeDtypeStruct((n // 2, count, lines, LANES), BF16)
    return pl.pallas_call(
        body,
        grid=(1,),
        in_specs=[smem_spec()]
        + [whole(part.shape) for part in grads]
        + [vmem_spec()] * 4
        + any_specs(2),
        out_specs=any_specs(1) + [vmem_spec()] * 4,
        out_shape=[pltpu.HBM((rows, n * width), BF16), wide, wide, messages, messages],
        scratch_shapes=[
            pltpu.VMEM((rows, n * width), BF16),
            pltpu.VMEM((rows, width), F32),
            *buffers(6, width, hidden_units),
            pltpu.SemaphoreType.DMA,
        ],
        compiler_params=params(32),
        cost_estimate=cost(
            (4 * n + 2 * (n - early)) * rows * width * hidden_units,
            4 * n * width * hidden_units,
        ),
        name="input_parts",
    )(
        index,
        *grads,
        grad_early,
        pltpu.with_memory_space_constraint(w_late, pltpu.VMEM),
        slope,
        silu,
        in_hbm(w_gate),
        in_hbm(w_up),
    )


def weight_grad(left, right, name):
    rows, out_rows = left.shape
    out_cols = right.shape[1]
    tile = min(512, out_rows)
    step = min(512, out_cols)

    def body(left_ref, right_ref, out_ref):
        for j in range(out_cols // step):
            cols = slice(j * step, (j + 1) * step)
            out_ref[0, :, cols] = dot(left_ref[...], right_ref[:, cols], 0, 0).astype(BF16)

    return pl.pallas_call(
        body,
        grid=(out_rows // tile,),
        in_specs=[
            pl.BlockSpec((rows, tile), lambda i: (0, i)),
            pl.BlockSpec((rows, out_cols), lambda i: (0, 0)),
        ],
        out_specs=pl.BlockSpec((1, tile, out_cols), lambda i: (0, i, 0)),
        out_shape=jax.ShapeDtypeStruct((1, out_rows, out_cols), BF16),
        compiler_params=params(32),
        cost_estimate=cost(4 * rows * out_rows * out_cols, 2 * out_rows * out_cols),
        name=name,
    )(left, right)


def tie(array, after):
    def body(array_ref, after_ref, out_ref):
        del array_ref, after_ref, out_ref

    return pl.pallas_call(
        body,
        in_specs=any_specs(2),
        out_specs=pl.BlockSpec(memory_space=pl.ANY),
        out_shape=jax.ShapeDtypeStruct(array.shape, array.dtype),
        input_output_aliases={0: 0},
        compiler_params=params(1),
        name="tie",
    )(array, after)


def across(array, distance, size):
    return lax.ppermute(array, "tensor", [(i, i ^ distance) for i in range(size)])


def exchange(messages):
    return lax.all_to_all(messages, "dp", split_axis=0, concat_axis=0, tiled=True)


def gather_parts(own, size, after=None):
    parts = [own] + [None] * (size - 1)
    for k in range(2, size, 2):
        parts[k] = across(own, k, size)
        if after is not None:
            parts[k] = tie(parts[k], after)
    for k in range(0, size, 2):
        parts[k + 1] = across(parts[k], 1, size)
    return parts


def shards(tokens, grad_out, expert_ids, gate_probs, w_gate, w_up, w_down):
    dp_size = lax.axis_size("dp")
    size = lax.axis_size("tensor")
    slices = dp_size // EXPERTS
    width = tokens.shape[1]
    rows = dp_size * CAP
    index = lax.axis_index("tensor").astype(jnp.int32).reshape(1)
    ids = expert_ids.T
    probs = gate_probs.T

    def spread(messages):
        return messages if slices == 1 else jnp.repeat(messages, slices, axis=0)

    early = 2
    token_messages, grad_messages = pack_messages(ids, probs, tokens, grad_out)
    token_parts = gather_parts(exchange(spread(token_messages)), size)
    own_grads = exchange(spread(grad_messages))
    first = gate_up_first(index, token_parts[:early], w_gate, w_up, rows, width)
    x, hidden, slope, silu = hidden_state(index, token_parts, first, w_gate, w_up, rows, width)
    grad_parts = gather_parts(tie(own_grads, first[0]), size, slope)
    grad_early, w_late = early_grads(
        index, grad_parts[:early], w_down, early, slope, rows, width
    )
    y, gate_grad, up_grad, odd, even = input_parts(
        index, grad_parts, early, grad_early, w_late, slope, silu, w_gate, w_up, rows, width
    )
    sums = even.astype(F32) + across(odd, 1, size).astype(F32)
    total = sums[-1]
    for i, k in enumerate(range(size - 2, 0, -2)):
        total = total + across(sums[i].astype(BF16), k, size).astype(F32)
    back = exchange(total.astype(BF16))
    grad_down = weight_grad(hidden, y, "down_grad")
    grad_gate = weight_grad(x, gate_grad, "gate_grad")
    grad_up = weight_grad(x, up_grad, "up_grad")
    by_slice = back.reshape((EXPERTS, slices) + back.shape[1:]).swapaxes(0, 1)
    input_grad = combine(ids, by_slice, slices, width)
    return (input_grad, grad_gate, grad_up, grad_down)


def solution(mesh):
    placed = (
        P("dp", "tensor"),
        P("dp", "tensor"),
        P("dp", None),
        P("dp", None),
        P("dp", None, "tensor"),
        P("dp", None, "tensor"),
        P("dp", "tensor", None),
    )
    return jax.shard_map(
        shards,
        mesh=mesh,
        in_specs=placed,
        out_specs=(
            P("dp", "tensor"),
            P("dp", None, "tensor"),
            P("dp", None, "tensor"),
            P("dp", "tensor", None),
        ),
        check_vma=False,
    )
```

```python
import functools

import jax
import jax.numpy as jnp
from jax import lax
from jax.experimental import pallas as pl
from jax.experimental.pallas import tpu as pltpu
from jax.sharding import PartitionSpec as P

EXPERTS = 8
TOP = 2
CAP = 33
MAIN = 32
LANES = 128
BF16 = jnp.bfloat16
F32 = jnp.float32
MIB = 1 << 20


def dot(left, right, left_dim, right_dim):
    return lax.dot_general(
        left, right, (((left_dim,), (right_dim,)), ((), ())), preferred_element_type=F32
    )


def message_rows(width):
    blocks = width // LANES
    return blocks * MAIN + -(-blocks // 8) * 8


def lanes(start):
    return pl.ds(pl.multiple_of(start, LANES), LANES)


def select_rows(ids):
    count = ids.shape[1]
    expert = lax.broadcasted_iota(jnp.int32, (EXPERTS, count), 0)
    hit = ids[0:1] == expert
    for choice in range(1, TOP):
        hit = hit | (ids[choice : choice + 1] == expert)
    earlier = lax.broadcasted_iota(jnp.int32, (count, count), 0) < lax.broadcasted_iota(
        jnp.int32, (count, count), 1
    )
    rank = dot(hit.astype(F32).astype(BF16), earlier.astype(F32).astype(BF16), 1, 0)
    rank = jnp.where(hit, rank, -1.0)
    place = lax.broadcasted_iota(jnp.int32, (MAIN, count), 0).astype(F32)
    rows = [(rank[e : e + 1] == place).astype(F32) for e in range(EXPERTS)]
    rows.append((rank == float(MAIN)).astype(F32))
    return jnp.concatenate(rows, axis=0)


def row_weights(ids, probs, picks):
    count = ids.shape[1]
    expert = lax.broadcasted_iota(jnp.int32, (EXPERTS, count), 0)
    weight = jnp.zeros((EXPERTS, count), F32)
    for choice in range(TOP):
        weight = weight + jnp.where(
            ids[choice : choice + 1] == expert, probs[choice : choice + 1], 0.0
        )
    spread = [jnp.broadcast_to(weight[e : e + 1], (MAIN, count)) for e in range(EXPERTS)]
    spread = jnp.concatenate(spread + [weight], axis=0)
    return jnp.sum(spread * picks, axis=1, keepdims=True)


def pack(out_ref, rows):
    count, width = out_ref.shape[0], rows.shape[1]
    blocks = width // LANES
    left = out_ref.shape[1] - blocks * MAIN
    for i in range(count):
        for c in range(blocks):
            piece = rows[i * MAIN : (i + 1) * MAIN, c * LANES : (c + 1) * LANES]
            out_ref[i, c * MAIN : (c + 1) * MAIN, :] = piece.astype(BF16)
        last = rows[count * MAIN + i : count * MAIN + i + 1]
        lines = [last[:, c * LANES : (c + 1) * LANES] for c in range(blocks)]
        lines.append(jnp.zeros((left - blocks, LANES), F32))
        out_ref[i, blocks * MAIN :, :] = jnp.concatenate(lines, axis=0).astype(BF16)


def unpack(out_ref, message_ref, width, start):
    count = message_ref.shape[0]
    blocks = width // LANES
    last = [message_ref[i, blocks * MAIN :, :].astype(F32) for i in range(count)]
    for c in range(blocks):
        place = lanes(start + c * LANES)
        for i in range(count):
            out_ref[i * MAIN : (i + 1) * MAIN, place] = message_ref[i, c * MAIN : (c + 1) * MAIN, :]
        lines = jnp.concatenate([piece[c : c + 1] for piece in last], axis=0)
        out_ref[count * MAIN :, place] = lines.astype(BF16)


def vmem_spec():
    return pl.BlockSpec(memory_space=pltpu.VMEM)


def smem_spec():
    return pl.BlockSpec(memory_space=pltpu.SMEM)


def params(mib):
    return pltpu.CompilerParams(vmem_limit_bytes=mib * MIB)


def cost(flops, nbytes):
    return pl.CostEstimate(flops=int(flops), bytes_accessed=int(nbytes), transcendentals=0)


def whole(shape):
    return pl.BlockSpec(shape, lambda i: (0,) * len(shape), pipeline_mode=pl.Buffered(1))


def in_hbm(array):
    return pltpu.with_memory_space_constraint(array, pltpu.HBM)


def pack_messages(ids, probs, tokens, grads):
    def body(ids_ref, probs_ref, tokens_ref, grads_ref, token_out, grad_out):
        ids_in = ids_ref[...]
        picks = select_rows(ids_in)
        scale = row_weights(ids_in, probs_ref[...], picks)
        picks = picks.astype(BF16)
        pack(token_out, dot(picks, tokens_ref[...], 1, 0))
        pack(grad_out, dot(picks, grads_ref[...], 1, 0) * scale)

    shape = (EXPERTS, message_rows(grads.shape[1]), LANES)
    arrays = (ids, probs, tokens, grads)
    return pl.pallas_call(
        body,
        grid=(1,),
        in_specs=[whole(array.shape) for array in arrays],
        out_specs=[whole(shape)] * 2,
        out_shape=[jax.ShapeDtypeStruct(shape, BF16)] * 2,
        compiler_params=params(8),
        name="pack_messages",
    )(*[in_hbm(array) for array in arrays])


def combine(ids, messages, slices, width):
    count = ids.shape[1]

    def body(ids_ref, message_ref, out_ref, rows_ref):
        picks = select_rows(ids_ref[...]).astype(BF16)
        total = jnp.zeros((count, width), F32)
        for s in range(slices):
            unpack(rows_ref, message_ref.at[s], width, 0)
            total = total + dot(picks, rows_ref[...], 0, 0)
        out_ref[...] = total.astype(BF16)

    return pl.pallas_call(
        body,
        in_specs=[vmem_spec()] * 2,
        out_specs=vmem_spec(),
        out_shape=jax.ShapeDtypeStruct((count, width), BF16),
        scratch_shapes=[pltpu.VMEM((EXPERTS * CAP, width), BF16)],
        compiler_params=params(16),
        name="combine",
    )(ids, messages)


IN_FLIGHT = 13 * MIB


class Stream:
    def __init__(self, *groups):
        self.copies, self.blocks, self.sizes, self.before = [], [], [], []
        for sources, held, sems in groups:
            slots, first = held.shape[0], len(self.copies)
            for i, source in enumerate(sources):
                slot = i % slots
                self.copies.append(
                    [
                        pltpu.make_async_copy(
                            source.at[:, cols], held.at[slot, :, cols], sems.at[slot, j]
                        )
                        for j, cols in enumerate(pieces(held.shape[2]))
                    ]
                )
                self.blocks.append(held.at[slot])
                self.sizes.append(2 * held.shape[1] * held.shape[2])
                self.before.append(first + i - slots if i >= slots else -1)
        self.started = self.arrived = self.used = 0
        self.start()

    def start(self):
        while self.started < len(self.copies):
            flying = sum(self.sizes[self.arrived : self.started + 1])
            if self.before[self.started] >= self.used or flying > IN_FLIGHT:
                break
            self.start_next()

    def start_next(self):
        for copy in self.copies[self.started]:
            copy.start()
        self.started += 1

    def next(self, count):
        self.used = self.arrived
        self.start()
        first = self.arrived
        for i in range(first, first + count):
            if i >= self.started:
                self.start_next()
            for copy in self.copies[i]:
                copy.wait()
        self.arrived += count
        self.start()
        return self.blocks[first : first + count]


PIECE = 4096


def pieces(columns):
    step = min(PIECE, columns)
    return [pl.ds(j, step) for j in range(0, columns, step)] if columns % step == 0 else [pl.ds(0, columns)]


def buffers(slots, *block):
    return [
        pltpu.VMEM((slots, *block), BF16),
        pltpu.SemaphoreType.DMA((slots, len(pieces(block[1])))),
    ]


def feature_block(ref, index, k, width, cols):
    start = pl.multiple_of((index ^ k) * width, LANES)
    return ref.at[0, pl.ds(start, width), cols]


def feature_cols(ref, index, k, width, rows):
    start = pl.multiple_of((index ^ k) * width, LANES)
    return ref.at[0, rows, pl.ds(start, width)]


def chunk_of(total):
    return min(512, total)


def chunks(total):
    step = chunk_of(total)
    return [pl.ds(j, step) for j in range(0, total, step)]


def any_specs(count):
    return [pl.BlockSpec(memory_space=pl.ANY)] * count


def gate_up_first(index, parts, w_gate, w_up, rows, width):
    hidden_units = w_gate.shape[2]
    n = len(parts)

    def body(index_ref, *refs):
        part_refs = refs[:n]
        w_gate_ref, w_up_ref, gate_ref, up_ref, x_ref, held_ref, sems = refs[n:]
        at = index_ref[0]
        sources = [
            feature_block(ref, at, k, width, cols)
            for cols in chunks(hidden_units)
            for ref in (w_gate_ref, w_up_ref)
            for k in range(n)
        ]
        stream = Stream((sources, held_ref, sems))
        for k in range(n):
            unpack(x_ref, part_refs[k], width, k * width)
        for cols in chunks(hidden_units):
            blocks = stream.next(2 * n)
            for i, out_ref in enumerate((gate_ref, up_ref)):
                value = None
                for k in range(n):
                    more = dot(x_ref[:, k * width : (k + 1) * width], blocks[i * n + k][...], 1, 0)
                    value = more if value is None else value + more
                out_ref[:, cols] = value

    wide = jax.ShapeDtypeStruct((rows, hidden_units), F32)
    return pl.pallas_call(
        body,
        in_specs=[smem_spec()] + [vmem_spec() for _ in parts] + any_specs(2),
        out_specs=[vmem_spec()] * 2,
        out_shape=[wide, wide],
        scratch_shapes=[
            pltpu.VMEM((rows, n * width), BF16),
            *buffers(6 * n, width, chunk_of(hidden_units)),
        ],
        compiler_params=params(20),
        cost_estimate=cost(
            4 * n * rows * width * hidden_units, 4 * n * width * hidden_units
        ),
        name="gate_up_first",
    )(index, *parts, in_hbm(w_gate), in_hbm(w_up))


def hidden_state(index, parts, gate_up, w_gate, w_up, rows, width):
    hidden_units = w_gate.shape[2]
    n = len(parts)
    early = 2
    late = n - early

    def body(index_ref, *refs):
        part_refs = refs[:n]
        gate_in, up_in, w_gate_ref, w_up_ref, x_ref, hidden_ref = refs[n : n + 6]
        slope_ref, silu_ref, held_ref, sems = refs[n + 6 :]
        at = index_ref[0]
        sources = [
            feature_block(ref, at, k, width, cols)
            for cols in chunks(hidden_units)
            for ref in (w_gate_ref, w_up_ref)
            for k in range(early, n)
        ]
        stream = Stream((sources, held_ref, sems))
        for k in range(n):
            unpack(x_ref, part_refs[k], width, (at ^ k) * width)
        for cols in chunks(hidden_units):
            values = []
            blocks = stream.next(2 * late)
            for i, before in enumerate((gate_in, up_in)):
                value = before[:, cols]
                for k in range(early, n):
                    place = pl.ds(pl.multiple_of((at ^ k) * width, LANES), width)
                    block = blocks[i * late + k - early]
                    value = value + dot(x_ref[:, place], block[...], 1, 0)
                values.append(value)
            gate, up = values
            sig = jax.nn.sigmoid(gate)
            silu = gate * sig
            hidden_ref[:, cols] = (silu * up).astype(BF16)
            slope_ref[:, cols] = (up * sig * (1.0 + gate * (1.0 - sig))).astype(BF16)
            silu_ref[:, cols] = silu.astype(BF16)

    wide = (rows, hidden_units)
    return pl.pallas_call(
        body,
        in_specs=[smem_spec()]
        + [vmem_spec() for _ in parts]
        + [vmem_spec()] * 2
        + any_specs(2),
        out_specs=[vmem_spec()] * 4,
        out_shape=[jax.ShapeDtypeStruct((rows, n * width), BF16)]
        + [jax.ShapeDtypeStruct(wide, BF16)] * 3,
        scratch_shapes=buffers(6 * late, width, chunk_of(hidden_units)),
        compiler_params=params(20),
        cost_estimate=cost(
            4 * late * rows * width * hidden_units, 4 * late * width * hidden_units
        ),
        name="hidden_state",
    )(index, *parts, *gate_up, in_hbm(w_gate), in_hbm(w_up))


def early_grads(index, parts, w_down, early, after, rows, width):
    hidden_units = w_down.shape[1]
    n = len(parts)
    late = w_down.shape[2] // width - early

    def body(index_ref, *refs):
        part_refs = refs[:n]
        w_down_ref, _, grad_ref, late_ref, y_ref, held_ref, sems, late_sems = refs[n:]
        at = index_ref[0]
        stream = Stream(
            (
                [
                    feature_cols(w_down_ref, at, k, width, cols)
                    for cols in chunks(hidden_units)
                    for k in range(early)
                ],
                held_ref,
                sems,
            )
        )
        copies = [
            pltpu.make_async_copy(
                feature_cols(w_down_ref, at, early + k, width, slice(None)),
                late_ref.at[k],
                late_sems.at[k],
            )
            for k in range(late)
        ]
        for k in range(n):
            unpack(y_ref, part_refs[k], width, k * width)
        for i, cols in enumerate(chunks(hidden_units)):
            blocks = stream.next(early)
            if i == 0:
                for copy in copies:
                    copy.start()
            value = None
            for k in range(early):
                more = dot(y_ref[:, k * width : (k + 1) * width], blocks[k][...], 1, 1)
                value = more if value is None else value + more
            grad_ref[:, cols] = value
        for copy in copies:
            copy.wait()

    return pl.pallas_call(
        body,
        in_specs=[smem_spec()] + [vmem_spec() for _ in parts] + any_specs(2),
        out_specs=[vmem_spec()] * 2,
        out_shape=[
            jax.ShapeDtypeStruct((rows, hidden_units), F32),
            pltpu.VMEM((late, hidden_units, width), BF16),
        ],
        scratch_shapes=[
            pltpu.VMEM((rows, early * width), BF16),
            *buffers(4 * early, chunk_of(hidden_units), width),
            pltpu.SemaphoreType.DMA((late,)),
        ],
        compiler_params=params(16),
        cost_estimate=cost(
            2 * early * rows * width * hidden_units, 4 * early * width * hidden_units
        ),
        name="early_grads",
    )(index, *parts, in_hbm(w_down), after)


def input_parts(index, grads, early, grad_early, w_late, slope, silu, w_gate, w_up, rows, width):
    hidden_units = w_gate.shape[2]
    n = len(grads)
    count, lines = grads[0].shape[:2]
    order = list(range(n - 1, 0, -2)) + list(range(n - 2, -1, -2))
    step = 256 if width % 256 == 0 else LANES

    def body(index_ref, *refs):
        part_refs = refs[:n]
        grad_in, late_ref, slope_ref, silu_ref, w_gate_ref, w_up_ref = refs[n : n + 6]
        y_ref, gate_ref, up_ref = refs[n + 6 : n + 9]
        out_refs, (rows_ref, held_ref, sems) = refs[n + 9 : -3], refs[-3:]
        at = index_ref[0]
        sources = [
            feature_block(ref, at, k, width, slice(None))
            for k in order
            for ref in (w_gate_ref, w_up_ref)
        ]
        stream = Stream((sources, held_ref, sems))
        for k in range(n):
            unpack(y_ref, part_refs[k], width, (at ^ k) * width)
        for cols in chunks(hidden_units):
            grad = grad_in[:, cols]
            for k in range(early, n):
                place = pl.ds(pl.multiple_of((at ^ k) * width, LANES), width)
                grad = grad + dot(y_ref[:, place], late_ref[k - early, cols, :], 1, 1)
            gate_ref[:, cols] = (grad * slope_ref[:, cols].astype(F32)).astype(BF16)
            up_ref[:, cols] = (grad * silu_ref[:, cols].astype(F32)).astype(BF16)

        def finish(i):
            pack(out_refs[i], rows_ref[i % 2])

        for i in range(n):
            gate_block, up_block = stream.next(2)
            for j in range(0, width, step):
                value = dot(gate_ref[...], gate_block[j : j + step, :], 1, 1)
                value = value + dot(up_ref[...], up_block[j : j + step, :], 1, 1)
                rows_ref[i % 2, :, j : j + step] = value
            if i > 0:
                finish(i - 1)
        finish(n - 1)

    wide = jax.ShapeDtypeStruct((rows, hidden_units), BF16)
    messages = jax.ShapeDtypeStruct((count, lines, LANES), BF16)
    return pl.pallas_call(
        body,
        in_specs=[smem_spec()]
        + [vmem_spec() for _ in grads]
        + [vmem_spec()] * 4
        + any_specs(2),
        out_specs=[vmem_spec()] * (3 + n),
        out_shape=[jax.ShapeDtypeStruct((rows, n * width), BF16), wide, wide] + [messages] * n,
        scratch_shapes=[
            pltpu.VMEM((2, rows, width), F32),
            *buffers(6, width, hidden_units),
        ],
        compiler_params=params(28),
        cost_estimate=cost(
            (4 * n + 2 * (n - early)) * rows * width * hidden_units,
            4 * n * width * hidden_units,
        ),
        name="input_parts",
    )(
        index,
        *grads,
        grad_early,
        pltpu.with_memory_space_constraint(w_late, pltpu.VMEM),
        slope,
        silu,
        in_hbm(w_gate),
        in_hbm(w_up),
    )


def weight_grads(left, rights, name):
    rows, out_rows = left.shape
    out_cols = rights[0].shape[1]
    n = len(rights)
    tile = min(512, out_rows)
    step = min(512, out_cols)

    def body(left_ref, *refs):
        for right_ref, out_ref in zip(refs[:n], refs[n:], strict=True):
            for j in range(out_cols // step):
                cols = slice(j * step, (j + 1) * step)
                out_ref[0, :, cols] = dot(left_ref[...], right_ref[:, cols], 0, 0).astype(BF16)

    return pl.pallas_call(
        body,
        grid=(out_rows // tile,),
        in_specs=[pl.BlockSpec((rows, tile), lambda i: (0, i))]
        + [pl.BlockSpec((rows, out_cols), lambda i: (0, 0))] * n,
        out_specs=[pl.BlockSpec((1, tile, out_cols), lambda i: (0, i, 0))] * n,
        out_shape=[jax.ShapeDtypeStruct((1, out_rows, out_cols), BF16)] * n,
        compiler_params=params(32),
        cost_estimate=cost(4 * n * rows * out_rows * out_cols, 2 * n * out_rows * out_cols),
        name=name,
    )(left, *rights)


def tie(array, after):
    def body(array_ref, after_ref, out_ref):
        del array_ref, after_ref, out_ref

    return pl.pallas_call(
        body,
        in_specs=any_specs(2),
        out_specs=pl.BlockSpec(memory_space=pl.ANY),
        out_shape=jax.ShapeDtypeStruct(array.shape, array.dtype),
        input_output_aliases={0: 0},
        compiler_params=params(1),
        name="tie",
    )(array, after)


def across(array, distance, size):
    return lax.ppermute(array, "tensor", [(i, i ^ distance) for i in range(size)])


def exchange(messages):
    return lax.all_to_all(messages, "dp", split_axis=0, concat_axis=0, tiled=True)


def far_parts(own, size, after):
    parts = []
    for k in range(2, size, 2):
        part = tie(across(own, k, size), after)
        parts += [part, across(part, 1, size)]
    return parts


def shards(tokens, grad_out, expert_ids, gate_probs, w_gate, w_up, w_down):
    dp_size = lax.axis_size("dp")
    size = lax.axis_size("tensor")
    slices = dp_size // EXPERTS
    width = tokens.shape[1]
    rows = dp_size * CAP
    index = lax.axis_index("tensor").astype(jnp.int32).reshape(1)
    ids = expert_ids.T
    probs = gate_probs.T

    def spread(messages):
        return messages if slices == 1 else jnp.repeat(messages, slices, axis=0)

    early = 2
    token_messages, grad_messages = pack_messages(ids, probs, tokens, grad_out)
    own_tokens = exchange(spread(token_messages))
    own_grads = exchange(spread(grad_messages))
    near_tokens = [own_tokens, across(own_tokens, 1, size)]
    first = gate_up_first(index, near_tokens, w_gate, w_up, rows, width)
    token_parts = near_tokens + far_parts(own_tokens, size, first[0])
    x, hidden, slope, silu = hidden_state(index, token_parts, first, w_gate, w_up, rows, width)
    own_grads = tie(own_grads, first[0])
    near_grads = [own_grads, across(own_grads, 1, size)]
    grad_early, w_late = early_grads(index, near_grads, w_down, early, slope, rows, width)
    grad_parts = near_grads + far_parts(own_grads, size, slope)
    y, gate_grad, up_grad, *parts = input_parts(
        index, grad_parts, early, grad_early, w_late, slope, silu, w_gate, w_up, rows, width
    )
    odd, even = parts[: size // 2], parts[size // 2 :]
    sums = [
        here.astype(F32) + across(there, 1, size).astype(F32)
        for here, there in zip(even, odd, strict=True)
    ]
    (grad_down,) = weight_grads(hidden, [y], "down_grad")
    total = sums[-1]
    for part, k in zip(sums[:-1], range(size - 2, 0, -2), strict=True):
        arrived = tie(across(part.astype(BF16), k, size), in_hbm(grad_down))
        total = total + arrived.astype(F32)
    back = exchange(total.astype(BF16))
    grad_gate, grad_up = weight_grads(in_hbm(x), [gate_grad, up_grad], "gate_up_grads")
    by_slice = back.reshape((EXPERTS, slices) + back.shape[1:]).swapaxes(0, 1)
    input_grad = combine(ids, by_slice, slices, width)
    return (input_grad, grad_gate, grad_up, grad_down)


def solution(mesh):
    placed = (
        P("dp", "tensor"),
        P("dp", "tensor"),
        P("dp", None),
        P("dp", None),
        P("dp", None, "tensor"),
        P("dp", None, "tensor"),
        P("dp", "tensor", None),
    )
    return jax.shard_map(
        shards,
        mesh=mesh,
        in_specs=placed,
        out_specs=(
            P("dp", "tensor"),
            P("dp", None, "tensor"),
            P("dp", None, "tensor"),
            P("dp", "tensor", None),
        ),
        check_vma=False,
    )
```

```python
import functools

import jax
import jax.numpy as jnp
from jax import lax
from jax.experimental import pallas as pl
from jax.experimental.pallas import tpu as pltpu
from jax.sharding import PartitionSpec as P

EXPERTS = 8
TOP = 2
CAP = 33
MAIN = 32
LANES = 128
BF16 = jnp.bfloat16
F32 = jnp.float32
MIB = 1 << 20


def dot(left, right, left_dim, right_dim):
    return lax.dot_general(
        left, right, (((left_dim,), (right_dim,)), ((), ())), preferred_element_type=F32
    )


def message_rows(width):
    blocks = width // LANES
    return blocks * MAIN + -(-blocks // 8) * 8


def lanes(start):
    return pl.ds(pl.multiple_of(start, LANES), LANES)


def select_rows(ids):
    count = ids.shape[1]
    expert = lax.broadcasted_iota(jnp.int32, (EXPERTS, count), 0)
    hit = ids[0:1] == expert
    for choice in range(1, TOP):
        hit = hit | (ids[choice : choice + 1] == expert)
    earlier = lax.broadcasted_iota(jnp.int32, (count, count), 0) < lax.broadcasted_iota(
        jnp.int32, (count, count), 1
    )
    rank = dot(hit.astype(F32).astype(BF16), earlier.astype(F32).astype(BF16), 1, 0)
    rank = jnp.where(hit, rank, -1.0)
    place = lax.broadcasted_iota(jnp.int32, (MAIN, count), 0).astype(F32)
    rows = [(rank[e : e + 1] == place).astype(F32) for e in range(EXPERTS)]
    rows.append((rank == float(MAIN)).astype(F32))
    return jnp.concatenate(rows, axis=0)


def row_weights(ids, probs, picks):
    count = ids.shape[1]
    expert = lax.broadcasted_iota(jnp.int32, (EXPERTS, count), 0)
    weight = jnp.zeros((EXPERTS, count), F32)
    for choice in range(TOP):
        weight = weight + jnp.where(
            ids[choice : choice + 1] == expert, probs[choice : choice + 1], 0.0
        )
    spread = [jnp.broadcast_to(weight[e : e + 1], (MAIN, count)) for e in range(EXPERTS)]
    spread = jnp.concatenate(spread + [weight], axis=0)
    return jnp.sum(spread * picks, axis=1, keepdims=True)


def pack(out_ref, rows):
    count, width = out_ref.shape[0], rows.shape[1]
    blocks = width // LANES
    left = out_ref.shape[1] - blocks * MAIN
    for i in range(count):
        for c in range(blocks):
            piece = rows[i * MAIN : (i + 1) * MAIN, c * LANES : (c + 1) * LANES]
            out_ref[i, c * MAIN : (c + 1) * MAIN, :] = piece.astype(BF16)
        last = rows[count * MAIN + i : count * MAIN + i + 1]
        lines = [last[:, c * LANES : (c + 1) * LANES] for c in range(blocks)]
        lines.append(jnp.zeros((left - blocks, LANES), F32))
        out_ref[i, blocks * MAIN :, :] = jnp.concatenate(lines, axis=0).astype(BF16)


def unpack(out_ref, message_ref, width, start):
    count = message_ref.shape[0]
    blocks = width // LANES
    last = [message_ref[i, blocks * MAIN :, :].astype(F32) for i in range(count)]
    for c in range(blocks):
        place = lanes(start + c * LANES)
        for i in range(count):
            out_ref[i * MAIN : (i + 1) * MAIN, place] = message_ref[i, c * MAIN : (c + 1) * MAIN, :]
        lines = jnp.concatenate([piece[c : c + 1] for piece in last], axis=0)
        out_ref[count * MAIN :, place] = lines.astype(BF16)


def vmem_spec():
    return pl.BlockSpec(memory_space=pltpu.VMEM)


def smem_spec():
    return pl.BlockSpec(memory_space=pltpu.SMEM)


def params(mib):
    return pltpu.CompilerParams(vmem_limit_bytes=mib * MIB)


def cost(flops, nbytes):
    return pl.CostEstimate(flops=int(flops), bytes_accessed=int(nbytes), transcendentals=0)


def whole(shape):
    return pl.BlockSpec(shape, lambda i: (0,) * len(shape), pipeline_mode=pl.Buffered(1))


def in_hbm(array):
    return pltpu.with_memory_space_constraint(array, pltpu.HBM)


def pack_tokens(ids, tokens):
    def body(ids_ref, tokens_ref, out_ref):
        picks = select_rows(ids_ref[...])
        pack(out_ref, dot(picks.astype(BF16), tokens_ref[...], 1, 0))

    shape = (EXPERTS, message_rows(tokens.shape[1]), LANES)
    arrays = (ids, tokens)
    return pl.pallas_call(
        body,
        grid=(1,),
        in_specs=[whole(array.shape) for array in arrays],
        out_specs=whole(shape),
        out_shape=jax.ShapeDtypeStruct(shape, BF16),
        compiler_params=params(8),
        name="pack_tokens",
    )(*[in_hbm(array) for array in arrays])


def pack_grads(ids, probs, grads):
    def body(ids_ref, probs_ref, grads_ref, out_ref):
        ids_in = ids_ref[...]
        picks = select_rows(ids_in)
        scale = row_weights(ids_in, probs_ref[...], picks)
        pack(out_ref, dot(picks.astype(BF16), grads_ref[...], 1, 0) * scale)

    shape = (EXPERTS, message_rows(grads.shape[1]), LANES)
    arrays = (ids, probs, grads)
    return pl.pallas_call(
        body,
        grid=(1,),
        in_specs=[whole(array.shape) for array in arrays],
        out_specs=whole(shape),
        out_shape=jax.ShapeDtypeStruct(shape, BF16),
        compiler_params=params(8),
        name="pack_grads",
    )(*[in_hbm(array) for array in arrays])


def combine(ids, messages, slices, width):
    count = ids.shape[1]

    def body(ids_ref, message_ref, out_ref, rows_ref):
        picks = select_rows(ids_ref[...]).astype(BF16)
        total = jnp.zeros((count, width), F32)
        for s in range(slices):
            unpack(rows_ref, message_ref.at[s], width, 0)
            total = total + dot(picks, rows_ref[...], 0, 0)
        out_ref[...] = total.astype(BF16)

    return pl.pallas_call(
        body,
        in_specs=[vmem_spec()] * 2,
        out_specs=vmem_spec(),
        out_shape=jax.ShapeDtypeStruct((count, width), BF16),
        scratch_shapes=[pltpu.VMEM((EXPERTS * CAP, width), BF16)],
        compiler_params=params(16),
        name="combine",
    )(ids, messages)


IN_FLIGHT = 13 * MIB


class Stream:
    def __init__(self, *groups):
        self.copies, self.blocks, self.sizes, self.before = [], [], [], []
        for sources, held, sems in groups:
            slots, first = held.shape[0], len(self.copies)
            for i, source in enumerate(sources):
                slot = i % slots
                self.copies.append(
                    [
                        pltpu.make_async_copy(
                            source.at[:, cols], held.at[slot, :, cols], sems.at[slot, j]
                        )
                        for j, cols in enumerate(pieces(held.shape[2]))
                    ]
                )
                self.blocks.append(held.at[slot])
                self.sizes.append(2 * held.shape[1] * held.shape[2])
                self.before.append(first + i - slots if i >= slots else -1)
        self.started = self.arrived = self.used = 0
        self.start()

    def start(self):
        while self.started < len(self.copies):
            flying = sum(self.sizes[self.arrived : self.started + 1])
            if self.before[self.started] >= self.used or flying > IN_FLIGHT:
                break
            self.start_next()

    def start_next(self):
        for copy in self.copies[self.started]:
            copy.start()
        self.started += 1

    def next(self, count):
        self.used = self.arrived
        self.start()
        first = self.arrived
        for i in range(first, first + count):
            if i >= self.started:
                self.start_next()
            for copy in self.copies[i]:
                copy.wait()
        self.arrived += count
        self.start()
        return self.blocks[first : first + count]


PIECE = 4096


def pieces(columns):
    step = min(PIECE, columns)
    return [pl.ds(j, step) for j in range(0, columns, step)] if columns % step == 0 else [pl.ds(0, columns)]


def buffers(slots, *block):
    return [
        pltpu.VMEM((slots, *block), BF16),
        pltpu.SemaphoreType.DMA((slots, len(pieces(block[1])))),
    ]


def feature_block(ref, index, k, width, cols):
    start = pl.multiple_of((index ^ k) * width, LANES)
    return ref.at[0, pl.ds(start, width), cols]


def feature_cols(ref, index, k, width, rows):
    start = pl.multiple_of((index ^ k) * width, LANES)
    return ref.at[0, rows, pl.ds(start, width)]


def chunk_of(total):
    return min(512, total)


def chunks(total):
    step = chunk_of(total)
    return [pl.ds(j, step) for j in range(0, total, step)]


def any_specs(count):
    return [pl.BlockSpec(memory_space=pl.ANY)] * count


def gate_up_first(index, parts, w_gate, w_up, rows, width):
    hidden_units = w_gate.shape[2]
    n = len(parts)

    def body(index_ref, *refs):
        part_refs = refs[:n]
        w_gate_ref, w_up_ref, gate_ref, up_ref, x_ref, held_ref, sems = refs[n:]
        at = index_ref[0]
        sources = [
            feature_block(ref, at, k, width, cols)
            for cols in chunks(hidden_units)
            for ref in (w_gate_ref, w_up_ref)
            for k in range(n)
        ]
        stream = Stream((sources, held_ref, sems))
        for k in range(n):
            unpack(x_ref, part_refs[k], width, k * width)
        for cols in chunks(hidden_units):
            blocks = stream.next(2 * n)
            for i, out_ref in enumerate((gate_ref, up_ref)):
                value = None
                for k in range(n):
                    more = dot(x_ref[:, k * width : (k + 1) * width], blocks[i * n + k][...], 1, 0)
                    value = more if value is None else value + more
                out_ref[:, cols] = value

    wide = jax.ShapeDtypeStruct((rows, hidden_units), F32)
    return pl.pallas_call(
        body,
        in_specs=[smem_spec()] + [vmem_spec() for _ in parts] + any_specs(2),
        out_specs=[vmem_spec()] * 2,
        out_shape=[wide, wide],
        scratch_shapes=[
            pltpu.VMEM((rows, n * width), BF16),
            *buffers(6 * n, width, chunk_of(hidden_units)),
        ],
        compiler_params=params(20),
        cost_estimate=cost(
            4 * n * rows * width * hidden_units, 4 * n * width * hidden_units
        ),
        name="gate_up_first",
    )(index, *parts, in_hbm(w_gate), in_hbm(w_up))


def hidden_state(index, parts, gate_up, w_gate, w_up, rows, width):
    hidden_units = w_gate.shape[2]
    n = len(parts)
    early = 2
    late = n - early

    def body(index_ref, *refs):
        part_refs = refs[:n]
        gate_in, up_in, w_gate_ref, w_up_ref, x_ref, hidden_ref = refs[n : n + 6]
        slope_ref, silu_ref, held_ref, sems = refs[n + 6 :]
        at = index_ref[0]
        sources = [
            feature_block(ref, at, k, width, cols)
            for cols in chunks(hidden_units)
            for ref in (w_gate_ref, w_up_ref)
            for k in range(early, n)
        ]
        stream = Stream((sources, held_ref, sems))
        for k in range(n):
            unpack(x_ref, part_refs[k], width, (at ^ k) * width)
        for cols in chunks(hidden_units):
            values = []
            blocks = stream.next(2 * late)
            for i, before in enumerate((gate_in, up_in)):
                value = before[:, cols]
                for k in range(early, n):
                    place = pl.ds(pl.multiple_of((at ^ k) * width, LANES), width)
                    block = blocks[i * late + k - early]
                    value = value + dot(x_ref[:, place], block[...], 1, 0)
                values.append(value)
            gate, up = values
            sig = jax.nn.sigmoid(gate)
            silu = gate * sig
            hidden_ref[:, cols] = (silu * up).astype(BF16)
            slope_ref[:, cols] = (up * sig * (1.0 + gate * (1.0 - sig))).astype(BF16)
            silu_ref[:, cols] = silu.astype(BF16)

    wide = (rows, hidden_units)
    return pl.pallas_call(
        body,
        in_specs=[smem_spec()]
        + [vmem_spec() for _ in parts]
        + [vmem_spec()] * 2
        + any_specs(2),
        out_specs=[vmem_spec()] * 4,
        out_shape=[jax.ShapeDtypeStruct((rows, n * width), BF16)]
        + [jax.ShapeDtypeStruct(wide, BF16)] * 3,
        scratch_shapes=buffers(6 * late, width, chunk_of(hidden_units)),
        compiler_params=params(20),
        cost_estimate=cost(
            4 * late * rows * width * hidden_units, 4 * late * width * hidden_units
        ),
        name="hidden_state",
    )(index, *parts, *gate_up, in_hbm(w_gate), in_hbm(w_up))


def early_grads(index, parts, w_down, early, after, rows, width):
    hidden_units = w_down.shape[1]
    n = len(parts)
    late = w_down.shape[2] // width - early

    def body(index_ref, *refs):
        part_refs = refs[:n]
        w_down_ref, _, grad_ref, late_ref, y_ref, held_ref, sems, late_sems = refs[n:]
        at = index_ref[0]
        stream = Stream(
            (
                [
                    feature_cols(w_down_ref, at, k, width, cols)
                    for cols in chunks(hidden_units)
                    for k in range(early)
                ],
                held_ref,
                sems,
            )
        )
        copies = [
            pltpu.make_async_copy(
                feature_cols(w_down_ref, at, early + k, width, slice(None)),
                late_ref.at[k],
                late_sems.at[k],
            )
            for k in range(late)
        ]
        for k in range(n):
            unpack(y_ref, part_refs[k], width, k * width)
        for i, cols in enumerate(chunks(hidden_units)):
            blocks = stream.next(early)
            if i == 0:
                for copy in copies:
                    copy.start()
            value = None
            for k in range(early):
                more = dot(y_ref[:, k * width : (k + 1) * width], blocks[k][...], 1, 1)
                value = more if value is None else value + more
            grad_ref[:, cols] = value
        for copy in copies:
            copy.wait()

    return pl.pallas_call(
        body,
        in_specs=[smem_spec()] + [vmem_spec() for _ in parts] + any_specs(2),
        out_specs=[vmem_spec()] * 2,
        out_shape=[
            jax.ShapeDtypeStruct((rows, hidden_units), F32),
            pltpu.VMEM((late, hidden_units, width), BF16),
        ],
        scratch_shapes=[
            pltpu.VMEM((rows, early * width), BF16),
            *buffers(4 * early, chunk_of(hidden_units), width),
            pltpu.SemaphoreType.DMA((late,)),
        ],
        compiler_params=params(16),
        cost_estimate=cost(
            2 * early * rows * width * hidden_units, 4 * early * width * hidden_units
        ),
        name="early_grads",
    )(index, *parts, in_hbm(w_down), after)


def input_parts(index, grads, early, grad_early, w_late, slope, silu, w_gate, w_up, rows, width):
    hidden_units = w_gate.shape[2]
    n = len(grads)
    count, lines = grads[0].shape[:2]
    order = list(range(n - 1, 0, -2)) + list(range(n - 2, -1, -2))
    step = 256 if width % 256 == 0 else LANES

    def body(index_ref, *refs):
        part_refs = refs[:n]
        grad_in, late_ref, slope_ref, silu_ref, w_gate_ref, w_up_ref = refs[n : n + 6]
        y_ref, gate_ref, up_ref = refs[n + 6 : n + 9]
        out_refs, (rows_ref, held_ref, sems) = refs[n + 9 : -3], refs[-3:]
        at = index_ref[0]
        sources = [
            feature_block(ref, at, k, width, slice(None))
            for k in order
            for ref in (w_gate_ref, w_up_ref)
        ]
        stream = Stream((sources, held_ref, sems))
        for k in range(n):
            unpack(y_ref, part_refs[k], width, (at ^ k) * width)
        for cols in chunks(hidden_units):
            grad = grad_in[:, cols]
            for k in range(early, n):
                place = pl.ds(pl.multiple_of((at ^ k) * width, LANES), width)
                grad = grad + dot(y_ref[:, place], late_ref[k - early, cols, :], 1, 1)
            gate_ref[:, cols] = (grad * slope_ref[:, cols].astype(F32)).astype(BF16)
            up_ref[:, cols] = (grad * silu_ref[:, cols].astype(F32)).astype(BF16)

        def finish(i):
            pack(out_refs[i], rows_ref[i % 2])

        for i in range(n):
            gate_block, up_block = stream.next(2)
            for j in range(0, width, step):
                value = dot(gate_ref[...], gate_block[j : j + step, :], 1, 1)
                value = value + dot(up_ref[...], up_block[j : j + step, :], 1, 1)
                rows_ref[i % 2, :, j : j + step] = value
            if i > 0:
                finish(i - 1)
        finish(n - 1)

    wide = jax.ShapeDtypeStruct((rows, hidden_units), BF16)
    messages = jax.ShapeDtypeStruct((count, lines, LANES), BF16)
    return pl.pallas_call(
        body,
        in_specs=[smem_spec()]
        + [vmem_spec() for _ in grads]
        + [vmem_spec()] * 4
        + any_specs(2),
        out_specs=[vmem_spec()] * (3 + n),
        out_shape=[jax.ShapeDtypeStruct((rows, n * width), BF16), wide, wide] + [messages] * n,
        scratch_shapes=[
            pltpu.VMEM((2, rows, width), F32),
            *buffers(6, width, hidden_units),
        ],
        compiler_params=params(28),
        cost_estimate=cost(
            (4 * n + 2 * (n - early)) * rows * width * hidden_units,
            4 * n * width * hidden_units,
        ),
        name="input_parts",
    )(
        index,
        *grads,
        grad_early,
        pltpu.with_memory_space_constraint(w_late, pltpu.VMEM),
        slope,
        silu,
        in_hbm(w_gate),
        in_hbm(w_up),
    )


def weight_grads(left, rights, name):
    rows, out_rows = left.shape
    out_cols = rights[0].shape[1]
    n = len(rights)
    tile = min(512, out_rows)
    step = min(512, out_cols)

    def body(left_ref, *refs):
        for right_ref, out_ref in zip(refs[:n], refs[n:], strict=True):
            for j in range(out_cols // step):
                cols = slice(j * step, (j + 1) * step)
                out_ref[0, :, cols] = dot(left_ref[...], right_ref[:, cols], 0, 0).astype(BF16)

    return pl.pallas_call(
        body,
        grid=(out_rows // tile,),
        in_specs=[pl.BlockSpec((rows, tile), lambda i: (0, i))]
        + [pl.BlockSpec((rows, out_cols), lambda i: (0, 0))] * n,
        out_specs=[pl.BlockSpec((1, tile, out_cols), lambda i: (0, i, 0))] * n,
        out_shape=[jax.ShapeDtypeStruct((1, out_rows, out_cols), BF16)] * n,
        compiler_params=params(32),
        cost_estimate=cost(4 * n * rows * out_rows * out_cols, 2 * n * out_rows * out_cols),
        name=name,
    )(left, *rights)


def tie(array, after):
    def body(array_ref, after_ref, out_ref):
        del array_ref, after_ref, out_ref

    return pl.pallas_call(
        body,
        in_specs=any_specs(2),
        out_specs=pl.BlockSpec(memory_space=pl.ANY),
        out_shape=jax.ShapeDtypeStruct(array.shape, array.dtype),
        input_output_aliases={0: 0},
        compiler_params=params(1),
        name="tie",
    )(array, after)


def across(array, distance, size):
    return lax.ppermute(array, "tensor", [(i, i ^ distance) for i in range(size)])


def exchange(messages):
    return lax.all_to_all(messages, "dp", split_axis=0, concat_axis=0, tiled=True)


def far_parts(own, size, after):
    parts = []
    for k in range(2, size, 2):
        part = tie(across(own, k, size), after)
        parts += [part, across(part, 1, size)]
    return parts


def shards(tokens, grad_out, expert_ids, gate_probs, w_gate, w_up, w_down):
    dp_size = lax.axis_size("dp")
    size = lax.axis_size("tensor")
    slices = dp_size // EXPERTS
    width = tokens.shape[1]
    rows = dp_size * CAP
    index = lax.axis_index("tensor").astype(jnp.int32).reshape(1)
    ids = expert_ids.T
    probs = gate_probs.T

    def spread(messages):
        return messages if slices == 1 else jnp.repeat(messages, slices, axis=0)

    early = 2
    grad_messages = pack_grads(ids, probs, grad_out)
    own_tokens = tie(exchange(spread(pack_tokens(ids, tokens))), grad_messages)
    own_grads = exchange(spread(grad_messages))
    near_tokens = [own_tokens, across(own_tokens, 1, size)]
    first = gate_up_first(index, near_tokens, w_gate, w_up, rows, width)
    token_parts = near_tokens + far_parts(own_tokens, size, first[0])
    x, hidden, slope, silu = hidden_state(index, token_parts, first, w_gate, w_up, rows, width)
    own_grads = tie(own_grads, first[0])
    near_grads = [own_grads, across(own_grads, 1, size)]
    grad_early, w_late = early_grads(index, near_grads, w_down, early, slope, rows, width)
    grad_parts = near_grads + far_parts(own_grads, size, slope)
    y, gate_grad, up_grad, *parts = input_parts(
        index, grad_parts, early, grad_early, w_late, slope, silu, w_gate, w_up, rows, width
    )
    odd, even = parts[: size // 2], parts[size // 2 :]
    sums = [
        here.astype(F32) + across(there, 1, size).astype(F32)
        for here, there in zip(even, odd, strict=True)
    ]
    grad_gate, grad_up = weight_grads(x, [gate_grad, up_grad], "gate_up_grads")
    total = sums[-1]
    for part, k in zip(sums[:-1], range(size - 2, 0, -2), strict=True):
        arrived = tie(across(part.astype(BF16), k, size), in_hbm(grad_gate))
        total = total + arrived.astype(F32)
    back = exchange(total.astype(BF16))
    (grad_down,) = weight_grads(in_hbm(hidden), [y], "down_grad")
    by_slice = back.reshape((EXPERTS, slices) + back.shape[1:]).swapaxes(0, 1)
    input_grad = combine(ids, by_slice, slices, width)
    return (input_grad, grad_gate, grad_up, grad_down)


def solution(mesh):
    placed = (
        P("dp", "tensor"),
        P("dp", "tensor"),
        P("dp", None),
        P("dp", None),
        P("dp", None, "tensor"),
        P("dp", None, "tensor"),
        P("dp", "tensor", None),
    )
    return jax.shard_map(
        shards,
        mesh=mesh,
        in_specs=placed,
        out_specs=(
            P("dp", "tensor"),
            P("dp", None, "tensor"),
            P("dp", None, "tensor"),
            P("dp", "tensor", None),
        ),
        check_vma=False,
    )
```
